32 devices in a mesh: row: 4 (over z), col: 8 (over y, x, core).
Axes of the slice: x: 2, y: 2, z: 4, core: 2. Of those that a mesh axis runs over, the one named last changes fastest.
Arguments:
- pair_counts: float32 [32, 32, 2, 128, 128], P(('row', 'col')), may hold values from 0.01 to 30
- tile_index: int32 [32, 32, 2], P(('row', 'col')), may hold values from 0 to 255
- slot_counts: int32 [32, 32], P(('row', 'col')), may hold values from 0 to 2, as said below
- row_totals: int32 [8192], P('row'), may hold values from 1000 to 59999
- col_totals: int32 [16384], P('col'), may hold values from 1000 to 59999
- sketch: bfloat16 [16384, 128], P('col'), may hold values from -0.046875 to 0.046875
Outputs:
- range_rows: bfloat16 [8192, 128], P('row')
- corange: bfloat16 [16384, 128], P('col')
The draws below stay inside these ranges and needn't reach their ends.
Inputs may be any that keep to these rules, and one draw needn't show every extreme that they name: `slot_counts`: slot counts from a shard to an owner; for some owners every shard fills all 2 slots. `tile_index`: tile positions may repeat; repeated tiles add.
All inputs are finite; a program needn't handle non-finite values.
Results may differ from the reference program's by a relative error of at most 0.001.
The reference program's roundings to bfloat16 on the way (of `pmi`) count: a program that leaves them out, or rounds other values in their place, can miss the bound.
Values may be sent and summed in bfloat16 or wider, within the bound.
A program may use at most 128 MiB of HBM per device.

```python
import math
import jax
import jax.numpy as jnp
from jax import lax

TILE = 128
SK = 128
CAP = 2
RT_DEV = 16
CT_DEV = 16
OWNERS = 32
ROWS = 8192
COLS = 16384
N_ROW = 4
N_COL = 8


def draw_slot_counts(key, part):
    first_key, second_key = jax.random.split(jax.random.fold_in(key, 17))
    order = jax.random.permutation(first_key, OWNERS)
    heavy = order < max(OWNERS // 8, 1)
    base = jax.random.randint(second_key, (OWNERS, OWNERS), 0, CAP + 1)
    return jnp.where(heavy[None, :], CAP, base).astype(jnp.int32)


def with_ends(result, stream_key, least, largest):
    extent = result.shape
    place = [jax.random.randint(jax.random.fold_in(stream_key, axis), (), 0, extent[axis]) for axis in range(len(extent))]
    result = result.at[tuple(place)].set(least)
    longest = extent.index(max(extent))
    place[longest] = (place[longest] + 1) % extent[longest]
    return result.at[tuple(place)].set(largest)


def level_of(own_key, shape, pieces, low, top_value):
    level, own = 1.0, jax.random.fold_in(own_key, 6)
    for dim, blocks in pieces:
        draws = jnp.exp(jax.random.uniform(jax.random.fold_in(own, dim), (blocks,), jnp.float32, low / len(pieces), top_value / len(pieces)))
        level = level * jnp.repeat(draws, shape[dim] // blocks).reshape([-1 if axis == dim else 1 for axis in range(len(shape))])
    return level


def normal_values(rng, dims, deviation, bound, cuts=(), kind=jnp.bfloat16):
    factor_of = level_of(rng, dims, cuts, -0.22, 0.18) if cuts else 1.0
    drawn = jax.random.normal(rng, dims, jnp.float32) * deviation * factor_of
    return jnp.minimum(jnp.maximum(drawn, -bound), bound).astype(kind)


def setup_inputs(seed: int = 0) -> dict:
    streams_of = jax.random.split(jax.random.key(seed), 7)
    pair_counts = jnp.clip(jnp.exp(math.log(30.0) - 8.006368 * jax.random.uniform(streams_of[0], (OWNERS, OWNERS, CAP, TILE, TILE), jnp.float32) ** level_of(streams_of[0], (OWNERS, OWNERS, CAP, TILE, TILE), ((0, 32),), -0.2, 0.2)), 0.01, 30.0)
    tile_index = with_ends(jax.random.randint(streams_of[1], (OWNERS, OWNERS, CAP), 0, RT_DEV * CT_DEV), jax.random.fold_in(streams_of[1], 1), 0, (RT_DEV * CT_DEV) - 1).astype(jnp.int32)
    slot_counts = draw_slot_counts(jax.random.fold_in(streams_of[6], 71), 0)
    row_totals = with_ends(jax.random.randint(streams_of[3], (ROWS,), 1000, 60000), jax.random.fold_in(streams_of[3], 1), 1000, 59999).astype(jnp.int32)
    col_totals = with_ends(jax.random.randint(streams_of[4], (COLS,), 1000, 60000), jax.random.fold_in(streams_of[4], 1), 1000, 59999).astype(jnp.int32)
    sketch = normal_values(streams_of[5], (COLS, SK), COLS ** -0.5, 0.046875, ((0, 8),))
    return {"pair_counts": pair_counts, "tile_index": tile_index, "slot_counts": slot_counts, "row_totals": row_totals, "col_totals": col_totals, "sketch": sketch}


log_shift = 0.25

def pmi_block(tiles, parked, row_here, col_here, grand):
    ntiles = RT_DEV * CT_DEV
    stack = jnp.zeros((ntiles + 1, TILE, TILE), jnp.float32).at[parked].add(tiles)[:ntiles]
    counts_block = stack.reshape(RT_DEV, CT_DEV, TILE, TILE).transpose(0, 2, 1, 3).reshape(RT_DEV * TILE, CT_DEV * TILE)
    scaled = counts_block * grand / (row_here.astype(jnp.float32)[:, None] * col_here.astype(jnp.float32)[None, :])
    return jnp.maximum(jnp.log1p(scaled) - log_shift, 0.0).astype(jnp.bfloat16)

def owner_pmi(owner, pair_counts, tile_index, slot_counts, row_totals, col_totals, grand):
    row_dev = (owner // N_COL).astype(jnp.int32)
    col_dev = (owner % N_COL).astype(jnp.int32)
    arrived = lax.dynamic_index_in_dim(pair_counts, owner, 1, keepdims=False)
    places = lax.dynamic_index_in_dim(tile_index, owner, 1, keepdims=False)
    filled = lax.dynamic_index_in_dim(slot_counts, owner, 1, keepdims=False)
    slots = lax.broadcasted_iota(jnp.int32, places.shape, 1)
    parked = jnp.where(slots < filled[:, None], places, RT_DEV * CT_DEV).astype(jnp.int32)
    row_here = lax.dynamic_slice_in_dim(row_totals, (row_dev * (RT_DEV * TILE)).astype(jnp.int32), RT_DEV * TILE)
    col_here = lax.dynamic_slice_in_dim(col_totals, (col_dev * (CT_DEV * TILE)).astype(jnp.int32), CT_DEV * TILE)
    pmi = pmi_block(arrived.reshape(-1, TILE, TILE), parked.reshape(-1), row_here, col_here, grand)
    return (pmi, row_dev, col_dev)

def reference(pair_counts, tile_index, slot_counts, row_totals, col_totals, sketch):
    grand = jnp.sum(row_totals.astype(jnp.float32))
    owners = jnp.arange(N_ROW * N_COL, dtype=jnp.int32)

    def first_pass(carry, owner):
        pmi, row_dev, col_dev = owner_pmi(owner, pair_counts, tile_index, slot_counts, row_totals, col_totals, grand)
        sketch_here = lax.dynamic_slice_in_dim(sketch, (col_dev * (CT_DEV * TILE)).astype(jnp.int32), CT_DEV * TILE, 0)
        product = jnp.dot(pmi, sketch_here, preferred_element_type=jnp.float32)
        return (carry.at[row_dev].add(product), None)
    row_sums, _ = lax.scan(first_pass, jnp.zeros((N_ROW, RT_DEV * TILE, SK), jnp.float32), owners)
    range_blocks = row_sums.astype(jnp.bfloat16)

    def second_pass(carry, owner):
        pmi, row_dev, col_dev = owner_pmi(owner, pair_counts, tile_index, slot_counts, row_totals, col_totals, grand)
        rows_here = lax.dynamic_index_in_dim(range_blocks, row_dev, 0, keepdims=False)
        product = lax.dot_general(pmi, rows_here, (((0,), (0,)), ((), ())), preferred_element_type=jnp.float32)
        return (carry.at[col_dev].add(product), None)
    col_sums, _ = lax.scan(second_pass, jnp.zeros((N_COL, CT_DEV * TILE, SK), jnp.float32), owners)
    range_rows = range_blocks.reshape(ROWS, SK)
    corange = (col_sums.reshape(COLS, SK) / math.sqrt(ROWS)).astype(jnp.bfloat16)
    return (range_rows, corange)
```

```python
import functools
import math

import jax
import jax.numpy as jnp
from jax import lax
from jax.experimental import pallas as pl
from jax.experimental.pallas import tpu as pltpu
from jax.sharding import PartitionSpec as P

TILE = 128
RT_DEV = 16
CT_DEV = 16
NT = RT_DEV * CT_DEV
SHIFT = 0.25
SCALE = 2.0**19
MESH = pl.DeviceIdType.MESH
VLIM = 56 * 1024 * 1024


def exchange_kernel(nr, nc, counts, meta, words_out, meta_out, send, sem_s, sem_r, msem_s, msem_r, lsem):
    n = nr * nc
    me = lax.axis_index("row") * nc + lax.axis_index("col")

    def pack(o):
        low = None
        for h in range(2):
            v = jnp.round(counts[o, h] * SCALE).astype(jnp.int32)
            send[o, h] = ((v >> 8) - 32768).astype(jnp.int16)
            part = v & 255
            low = part if h == 0 else low + (part << 8)
        send[o, 2] = (low - 32768).astype(jnp.int16)

    def copies(d):
        o = lax.rem(me + d, n)
        to = (o // nc, lax.rem(o, nc))
        return (
            pltpu.make_async_remote_copy(
                src_ref=send.at[o], dst_ref=words_out.at[me], send_sem=sem_s.at[d],
                recv_sem=sem_r.at[d], device_id=to, device_id_type=MESH),
            pltpu.make_async_remote_copy(
                src_ref=meta.at[o], dst_ref=meta_out.at[me], send_sem=msem_s.at[d],
                recv_sem=msem_r.at[d], device_id=to, device_id_type=MESH),
        )

    def issue(i, _):
        d = i + 1
        pack(lax.rem(me + d, n))
        a, b = copies(d)
        a.start()
        b.start()
        return 0

    lax.fori_loop(0, n - 1, issue, 0)
    pack(me)
    own = pltpu.make_async_copy(send.at[me], words_out.at[me], lsem.at[0])
    own_meta = pltpu.make_async_copy(meta.at[me], meta_out.at[me], lsem.at[1])
    own.start()
    own_meta.start()

    def finish(i, _):
        a, b = copies(i + 1)
        a.wait()
        b.wait()
        return 0

    lax.fori_loop(0, n - 1, finish, 0)
    own.wait()
    own_meta.wait()


def pmi_kernel(nr, nc, meta, words, row_tot, col_tot, out, acc, row_f, col_f, seen):
    n = nr * nc

    def clear(i, _):
        seen[i] = 0
        return 0

    lax.fori_loop(0, NT, clear, 0)
    total = lax.fori_loop(0, nr, lambda a, t: t + meta[a * nc * 3 + 2], jnp.int32(0))
    grand = total.astype(jnp.float32)
    col_f[...] = (1.0 / SCALE) / col_tot[...].astype(jnp.float32)

    def rows(i, _):
        r = row_tot[pl.ds(i, 1), :].astype(jnp.float32)
        f = jnp.broadcast_to(grand / r, (TILE, TILE))
        row_f[pl.ds(i * TILE, TILE), :] = f.T
        return 0

    lax.fori_loop(0, RT_DEV, rows, 0)

    def add(s, _):
        for h in range(2):
            p = meta[s * 3 + h]

            @pl.when(p < NT)
            def _():
                low = words[s, 2].astype(jnp.int32) + 32768
                low = (low & 255) if h == 0 else (low >> 8)
                v = (words[s, h].astype(jnp.int32) + 32768) * 256 + low
                before = seen[p]

                @pl.when(before == 0)
                def _():
                    acc[p] = v

                @pl.when(before != 0)
                def _():
                    acc[p] = acc[p] + v

                seen[p] = 1

        return 0

    lax.fori_loop(0, n, add, 0)

    def tile(p, _):
        tr = p // CT_DEV
        tc = lax.rem(p, CT_DEV)
        rs = pl.ds(pl.multiple_of(tr * TILE, TILE), TILE)
        cs = pl.ds(pl.multiple_of(tc * TILE, TILE), TILE)

        @pl.when(seen[p] == 0)
        def _():
            out[rs, cs] = jnp.zeros((TILE, TILE), jnp.bfloat16)

        @pl.when(seen[p] != 0)
        def _():
            x = acc[p].astype(jnp.float32) * row_f[rs, :] * col_f[pl.ds(tc, 1), :]
            out[rs, cs] = jnp.maximum(jnp.log1p(x) - SHIFT, 0.0).astype(jnp.bfloat16)

        return 0

    lax.fori_loop(0, NT, tile, 0)


def sketch_kernel(nr, nc, inv, pmi, sketch, rr_out, co_out, p1, r1, rr, acc, p2, r2, co,
                  s1s, s1r, s2s, s2r, s3s, s3r, s4s, s4r):
    my_r = lax.axis_index("row")
    my_c = lax.axis_index("col")
    ch = pmi.shape[0] // nc
    cz = pmi.shape[1] // nr

    def rows_of(j):
        return pl.ds(pl.multiple_of(j * ch, ch), ch)

    def cols_of(j):
        return pl.ds(pl.multiple_of(j * cz, cz), cz)

    def rs_col(d):
        return pltpu.make_async_remote_copy(
            src_ref=p1.at[d], dst_ref=r1.at[d], send_sem=s1s.at[d], recv_sem=s1r.at[d],
            device_id=(my_r, lax.rem(my_c + d, nc)), device_id_type=MESH)

    def ag_col(d):
        return pltpu.make_async_remote_copy(
            src_ref=rr.at[rows_of(my_c)], dst_ref=rr.at[rows_of(my_c)], send_sem=s2s.at[d],
            recv_sem=s2r.at[d], device_id=(my_r, lax.rem(my_c + d, nc)), device_id_type=MESH)

    def rs_row(d):
        return pltpu.make_async_remote_copy(
            src_ref=p2.at[d], dst_ref=r2.at[d], send_sem=s3s.at[d], recv_sem=s3r.at[d],
            device_id=(lax.rem(my_r + d, nr), my_c), device_id_type=MESH)

    def ag_row(d):
        return pltpu.make_async_remote_copy(
            src_ref=co.at[cols_of(my_r)], dst_ref=co.at[cols_of(my_r)], send_sem=s4s.at[d],
            recv_sem=s4r.at[d], device_id=(lax.rem(my_r + d, nr), my_c), device_id_type=MESH)

    def product(j):
        return jnp.dot(pmi[rows_of(j), :], sketch[...], preferred_element_type=jnp.float32)

    def first(i, _):
        d = i + 1
        p1[d] = product(lax.rem(my_c + d, nc))
        rs_col(d).start()
        return 0

    lax.fori_loop(0, nc - 1, first, 0)
    p1[0] = product(my_c)

    def gather(i, _):
        rs_col(i + 1).wait()
        p1[0] = p1[0] + r1[i + 1]
        return 0

    lax.fori_loop(0, nc - 1, gather, 0)
    rr[rows_of(my_c), :] = p1[0].astype(jnp.bfloat16)

    def spread(i, _):
        ag_col(i + 1).start()
        return 0

    lax.fori_loop(0, nc - 1, spread, 0)

    def turned(j):
        left = rr[rows_of(j), :].astype(jnp.float32).T.astype(jnp.bfloat16)
        return jnp.dot(left, pmi[rows_of(j), :], preferred_element_type=jnp.float32)

    acc[...] = turned(my_c)

    def second(i, _):
        ag_col(i + 1).wait_recv()
        acc[...] += turned(lax.rem(my_c - (i + 1) + nc, nc))
        return 0

    lax.fori_loop(0, nc - 1, second, 0)

    def third(i, _):
        d = i + 1
        p2[d] = acc[:, cols_of(lax.rem(my_r + d, nr))].T
        rs_row(d).start()
        return 0

    lax.fori_loop(0, nr - 1, third, 0)
    p2[0] = acc[:, cols_of(my_r)].T

    def sent(i, _):
        ag_col(i + 1).wait_send()
        return 0

    lax.fori_loop(0, nc - 1, sent, 0)
    rr_out[...] = rr[...]

    def fourth(i, _):
        rs_row(i + 1).wait()
        p2[0] = p2[0] + r2[i + 1]
        return 0

    lax.fori_loop(0, nr - 1, fourth, 0)
    co[cols_of(my_r), :] = (p2[0] * inv).astype(jnp.bfloat16)

    def fifth(i, _):
        ag_row(i + 1).start()
        return 0

    lax.fori_loop(0, nr - 1, fifth, 0)

    def sixth(i, _):
        ag_row(i + 1).wait()
        return 0

    lax.fori_loop(0, nr - 1, sixth, 0)
    co_out[...] = co[...]


def on_device(nr, nc, pair_counts, tile_index, slot_counts, row_totals, col_totals, sketch):
    n = nr * nc
    vm = pl.BlockSpec(memory_space=pltpu.VMEM)
    dma = pltpu.SemaphoreType.DMA
    slots = lax.broadcasted_iota(jnp.int32, tile_index.shape, 2)
    parked = jnp.where(slots < slot_counts[:, :, None], tile_index, NT)[0]
    part = jnp.broadcast_to(jnp.sum(row_totals), (n, 6))
    meta = jnp.concatenate([parked, part], axis=1)
    meta = jnp.broadcast_to(meta[:, :, None], (n, 8, TILE)).astype(jnp.int32)
    words, meta = pl.pallas_call(
        functools.partial(exchange_kernel, nr, nc),
        out_shape=(
            jax.ShapeDtypeStruct((n, 3, TILE, TILE), jnp.int16),
            jax.ShapeDtypeStruct((n, 8, TILE), jnp.int32),
        ),
        in_specs=[vm, vm],
        out_specs=(pl.BlockSpec(memory_space=pl.ANY), pl.BlockSpec(memory_space=pl.ANY)),
        scratch_shapes=[pltpu.VMEM((n, 3, TILE, TILE), jnp.int16)]
        + [dma((n,))] * 4 + [dma((2,))],
        compiler_params=pltpu.CompilerParams(has_side_effects=True, vmem_limit_bytes=VLIM),
        name="exchange",
    )(pair_counts[0], meta)
    pmi = pl.pallas_call(
        functools.partial(pmi_kernel, nr, nc),
        out_shape=jax.ShapeDtypeStruct((RT_DEV * TILE, CT_DEV * TILE), jnp.bfloat16),
        in_specs=[pl.BlockSpec(memory_space=pltpu.SMEM), vm, vm, vm],
        out_specs=vm,
        scratch_shapes=[
            pltpu.VMEM((NT, TILE, TILE), jnp.int32),
            pltpu.VMEM((RT_DEV * TILE, TILE), jnp.float32),
            pltpu.VMEM((CT_DEV, TILE), jnp.float32),
            pltpu.SMEM((NT,), jnp.int32),
        ],
        compiler_params=pltpu.CompilerParams(vmem_limit_bytes=VLIM),
        name="pmi",
    )(
        meta[:, :3, 0].reshape(-1),
        words,
        row_totals.reshape(RT_DEV, TILE),
        col_totals.reshape(CT_DEV, TILE),
    )
    rows, cols = pmi.shape
    sk = sketch.shape[1]
    ch, cz = rows // nc, cols // nr
    f32, bf16 = jnp.float32, jnp.bfloat16
    return pl.pallas_call(
        functools.partial(sketch_kernel, nr, nc, 1.0 / math.sqrt(rows * nr)),
        out_shape=(
            jax.ShapeDtypeStruct((rows, sk), bf16),
            jax.ShapeDtypeStruct((cols, sk), bf16),
        ),
        in_specs=[vm, vm],
        out_specs=(vm, vm),
        scratch_shapes=[
            pltpu.VMEM((nc, ch, sk), f32),
            pltpu.VMEM((nc, ch, sk), f32),
            pltpu.VMEM((rows, sk), bf16),
            pltpu.VMEM((sk, cols), f32),
            pltpu.VMEM((nr, cz, sk), f32),
            pltpu.VMEM((nr, cz, sk), f32),
            pltpu.VMEM((cols, sk), bf16),
        ]
        + [dma((nc,))] * 4 + [dma((nr,))] * 4,
        compiler_params=pltpu.CompilerParams(has_side_effects=True, vmem_limit_bytes=VLIM),
        name="sketch",
    )(pmi, sketch)


def solution(mesh):
    placed = (
        P(("row", "col"), None, None, None, None),
        P(("row", "col"), None, None),
        P(("row", "col"), None),
        P("row"),
        P("col"),
        P("col", None),
    )
    return jax.shard_map(
        functools.partial(on_device, mesh.shape["row"], mesh.shape["col"]),
        mesh=mesh,
        in_specs=placed,
        out_specs=(P("row", None), P("col", None)),
        check_vma=False,
    )
```

```python
import functools
import math

import jax
import jax.numpy as jnp
from jax import lax
from jax.experimental import pallas as pl
from jax.experimental.pallas import tpu as pltpu
from jax.sharding import PartitionSpec as P

TILE = 128
RT_DEV = 16
CT_DEV = 16
NT = RT_DEV * CT_DEV
HALF = TILE // 2
SHIFT = 0.25
CODE = 1048570.0 / math.sqrt(30.0)
TOP = 32766.0
MESH = pl.DeviceIdType.MESH
MIB = 1024 * 1024


def exchange_kernel(nr, nc, counts, places, used, row_tot, words_out, meta_out,
                    send, meta, sem_s, sem_r, msem_s, msem_r, lsem):
    n = nr * nc
    hr = nr // 2
    my_r = lax.axis_index("row")
    my_c = lax.axis_index("col")
    me = my_r * nc + my_c
    part = jnp.sum(row_tot[...])
    lane = lax.broadcasted_iota(jnp.int32, (1, TILE), 1)

    def pack(o):
        low = None
        for h in range(2):
            y = counts[o, h]
            r = lax.rsqrt(y)
            t = y * r
            t = t + 0.5 * r * (y - t * t)
            v = jnp.round(t * CODE).astype(jnp.int32)
            send[o, h * TILE : (h + 1) * TILE] = ((v >> 4) - 32768).astype(jnp.int16)
            v = v & 15
            v = v[:HALF] + (v[HALF:] << 4)
            low = v if h == 0 else low + (v << 8)
        send[o, 2 * TILE :] = (low - 32768).astype(jnp.int16)
        k = jnp.where(lane == 2, used[0, o], part)
        k = jnp.where(lane == 1, places[1, o], k)
        meta[o] = jnp.where(lane == 0, places[0, o], k)

    def target(i):
        q = i // 2
        side = lax.rem(my_r // hr + 1 + lax.rem(i, 2), 2)
        row = side * hr + lax.rem(my_r + q // nc, hr)
        return row, lax.rem(my_c + lax.rem(q, nc), nc)

    def copies(i):
        row, col = target(i)
        o = row * nc + col
        return o, (
            pltpu.make_async_remote_copy(
                src_ref=send.at[o], dst_ref=words_out.at[me], send_sem=sem_s.at[i],
                recv_sem=sem_r.at[i], device_id=(row, col), device_id_type=MESH),
            pltpu.make_async_remote_copy(
                src_ref=meta.at[o], dst_ref=meta_out.at[me], send_sem=msem_s.at[i],
                recv_sem=msem_r.at[i], device_id=(row, col), device_id_type=MESH),
        )

    def issue(i, _):
        o, (a, b) = copies(i)
        pack(o)
        a.start()
        b.start()
        return 0

    def finish(i, _):
        _, (a, b) = copies(i)
        a.wait()
        b.wait()
        return 0

    issue(0, 0)
    lax.fori_loop(2, n, issue, 0)
    pack(me)
    own = pltpu.make_async_copy(send.at[me], words_out.at[me], lsem.at[0])
    own_meta = pltpu.make_async_copy(meta.at[me], meta_out.at[me], lsem.at[1])
    own.start()
    own_meta.start()
    finish(0, 0)
    lax.fori_loop(2, n, finish, 0)
    own.wait()
    own_meta.wait()


def pmi_kernel(nr, nc, meta, words, row_tot, col_tot, out, acc, row_f, col_f, seen):
    n = nr * nc

    def clear(i, _):
        seen[i] = 0
        return 0

    lax.fori_loop(0, NT, clear, 0)
    total = lax.fori_loop(0, nr, lambda a, t: t + meta[a * nc, 0, 3], jnp.int32(0))
    grand = total.astype(jnp.float32)
    col_f[...] = (1.0 / (CODE * CODE)) / col_tot[...].astype(jnp.float32)

    def rows(i, _):
        r = row_tot[pl.ds(i, 1), :].astype(jnp.float32)
        f = jnp.broadcast_to(grand / r, (TILE, TILE))
        row_f[pl.ds(i * TILE, TILE), :] = f.T
        return 0

    lax.fori_loop(0, RT_DEV, rows, 0)

    def add(s, _):
        for h in range(2):
            p = meta[s, 0, h]

            @pl.when(h < meta[s, 0, 2])
            def _():
                low = (words[s, 2 * TILE :].astype(jnp.int32) + 32768) >> (8 * h)
                fresh = seen[p] == 0
                for g in range(2):
                    at = slice(g * HALF, (g + 1) * HALF)
                    from_ = slice(h * TILE + g * HALF, h * TILE + (g + 1) * HALF)
                    v = (words[s, from_].astype(jnp.int32) + 32768) * 16
                    v = (v + ((low >> (4 * g)) & 15)).astype(jnp.float32)
                    v = v * v

                    @pl.when(fresh)
                    def _():
                        acc[p, at] = v

                    @pl.when(jnp.logical_not(fresh))
                    def _():
                        acc[p, at] = acc[p, at] + v

                seen[p] = 1

        return 0

    lax.fori_loop(0, n, add, 0)

    def tile(p, _):
        tr = p // CT_DEV
        tc = lax.rem(p, CT_DEV)
        rs = pl.ds(pl.multiple_of(tr * TILE, TILE), TILE)
        cs = pl.ds(pl.multiple_of(tc * TILE, TILE), TILE)

        @pl.when(seen[p] == 0)
        def _():
            out[rs, cs] = jnp.zeros((TILE, TILE), jnp.bfloat16)

        @pl.when(seen[p] != 0)
        def _():
            x = acc[p] * row_f[rs, :] * col_f[pl.ds(tc, 1), :]
            out[rs, cs] = jnp.maximum(jnp.log(1.0 + x) - SHIFT, 0.0).astype(jnp.bfloat16)

        return 0

    lax.fori_loop(0, NT, tile, 0)


def sketch_kernel(nr, nc, inv, pmi, sketch, rr_out, co_out, pa, ra, p1, r1, rr, acc, p2, r2,
                  f2, g2, co, sas, sar, s1s, s1r, s2s, s2r, sfs, sfr, s3s, s3r, s5s, s5r,
                  s4s, s4r):
    my_r = lax.axis_index("row")
    my_c = lax.axis_index("col")
    nk = nc // 2
    k = my_c // 2
    core = lax.rem(my_c, 2)
    other = 1 - core
    ch = pmi.shape[0] // nc
    cz = pmi.shape[1] // nr

    def rows_of(j):
        return pl.ds(pl.multiple_of(j * ch, ch), ch)

    def cols_of(j):
        return pl.ds(pl.multiple_of(j * cz, cz), cz)

    def remote(src, dst, a, b, to):
        return pltpu.make_async_remote_copy(
            src_ref=src, dst_ref=dst, send_sem=a, recv_sem=b, device_id=to,
            device_id_type=MESH)

    sibling = (my_r, k * 2 + other)

    def chip(d):
        return (my_r, lax.rem(k + d, nk) * 2 + core)

    def to_sibling(d):
        return remote(pa.at[d], ra.at[d], sas.at[d], sar.at[d], sibling)

    def rs_col(d):
        return remote(p1.at[d], r1.at[d], s1s.at[d], s1r.at[d], chip(d))

    def ag_col(d):
        mine = rr.at[rows_of(my_c)]
        return remote(mine, mine, s2s.at[d], s2r.at[d], chip(d))

    def origin(d):
        return lax.rem(k - d + nk, nk) * 2

    def forward(d):
        block = rr.at[rows_of(origin(d) + core)]
        return remote(block, block, sfs.at[d], sfr.at[d], sibling)

    def row_peer(d):
        return (lax.rem(my_r + d, nr), my_c)

    def rs_row(d):
        return (
            remote(p2.at[d], r2.at[d], s3s.at[d], s3r.at[d], row_peer(d)),
            remote(f2.at[d], g2.at[d], s5s.at[d], s5r.at[d], row_peer(d)),
        )

    def ag_row(d):
        mine = co.at[cols_of(my_r)]
        return remote(mine, mine, s4s.at[d], s4r.at[d], row_peer(d))

    def product(j):
        return jnp.dot(pmi[rows_of(j), :], sketch[...], preferred_element_type=jnp.float32)

    def zeroth(i, _):
        d = lax.rem(i + 1, nk)
        pa[d] = product(lax.rem(k + d, nk) * 2 + other)
        to_sibling(d).start()
        return 0

    lax.fori_loop(0, nk, zeroth, 0)

    def first(i, _):
        d = i + 1
        mine = product(lax.rem(k + d, nk) * 2 + core)
        to_sibling(d).wait_recv()
        p1[d] = mine + ra[d]
        rs_col(d).start()
        return 0

    lax.fori_loop(0, nk - 1, first, 0)
    own = product(my_c)
    to_sibling(0).wait_recv()
    p1[0] = own + ra[0]

    def gather(i, _):
        rs_col(i + 1).wait_recv()
        p1[0] = p1[0] + r1[i + 1]
        return 0

    lax.fori_loop(0, nk - 1, gather, 0)
    rr[rows_of(my_c), :] = p1[0].astype(jnp.bfloat16)

    def spread(i, _):
        ag_col(i + 1).start()
        return 0

    lax.fori_loop(0, nk - 1, spread, 0)
    forward(0).start()

    def turned(j):
        left = rr[rows_of(j), :].astype(jnp.float32).T.astype(jnp.bfloat16)
        return jnp.dot(left, pmi[rows_of(j), :], preferred_element_type=jnp.float32)

    acc[...] = turned(my_c)
    forward(0).wait_recv()
    acc[...] += turned(k * 2 + other)

    def second(i, _):
        d = i + 1
        ag_col(d).wait_recv()
        forward(d).start()
        acc[...] += turned(origin(d) + core)
        forward(d).wait_recv()
        acc[...] += turned(origin(d) + other)
        return 0

    lax.fori_loop(0, nk - 1, second, 0)

    def third(i, _):
        d = i + 1
        a = acc[:, cols_of(lax.rem(my_r + d, nr))]
        m = jnp.max(jnp.abs(a), axis=0, keepdims=True)
        up = jnp.where(m > 1e-30, TOP / jnp.maximum(m, 1e-30), 0.0)
        p2[d] = jnp.round(a * up).astype(jnp.int32).astype(jnp.int16)
        f2[d] = jnp.broadcast_to(m * (1.0 / TOP), (8, cz))
        a, b = rs_row(d)
        a.start()
        b.start()
        return 0

    lax.fori_loop(0, nr - 1, third, 0)

    def sent(i, _):
        d = i + 1
        rs_col(d).wait_send()
        ag_col(d).wait_send()
        to_sibling(d).wait_send()
        forward(d).wait_send()
        return 0

    lax.fori_loop(0, nk - 1, sent, 0)
    to_sibling(0).wait_send()
    forward(0).wait_send()
    rr_out[...] = rr[...]
    mine = cols_of(my_r)

    def fourth(i, _):
        d = i + 1
        a, b = rs_row(d)
        a.wait()
        b.wait()
        acc[:, mine] += r2[d].astype(jnp.int32).astype(jnp.float32) * g2[d, 0:1, :]
        return 0

    lax.fori_loop(0, nr - 1, fourth, 0)
    co[mine, :] = (acc[:, mine].T * inv).astype(jnp.bfloat16)

    def fifth(i, _):
        ag_row(i + 1).start()
        return 0

    lax.fori_loop(0, nr - 1, fifth, 0)

    def sixth(i, _):
        ag_row(i + 1).wait()
        return 0

    lax.fori_loop(0, nr - 1, sixth, 0)
    co_out[...] = co[...]


def on_device(nr, nc, pair_counts, tile_index, slot_counts, row_totals, col_totals, sketch):
    n = nr * nc
    vm = pl.BlockSpec(memory_space=pltpu.VMEM)
    sm = pl.BlockSpec(memory_space=pltpu.SMEM)
    hbm = pl.BlockSpec(memory_space=pl.ANY)
    dma = pltpu.SemaphoreType.DMA
    f32, bf16, i16, i32 = jnp.float32, jnp.bfloat16, jnp.int16, jnp.int32
    row_tot = row_totals.reshape(RT_DEV, TILE)
    words_rows = 2 * TILE + HALF
    words, meta = pl.pallas_call(
        functools.partial(exchange_kernel, nr, nc),
        out_shape=(
            jax.ShapeDtypeStruct((n, words_rows, TILE), i16),
            jax.ShapeDtypeStruct((n, 1, TILE), i32),
        ),
        in_specs=[vm, sm, sm, vm],
        out_specs=(hbm, hbm),
        scratch_shapes=[pltpu.VMEM((n, words_rows, TILE), i16), pltpu.VMEM((n, 1, TILE), i32)]
        + [dma((n,))] * 4 + [dma((2,))],
        compiler_params=pltpu.CompilerParams(
            has_side_effects=True, vmem_limit_bytes=8 * MIB + n * MIB // 4),
        name="exchange",
    )(pair_counts[0], tile_index[0].T, slot_counts, row_tot)
    pmi = pl.pallas_call(
        functools.partial(pmi_kernel, nr, nc),
        out_shape=jax.ShapeDtypeStruct((RT_DEV * TILE, CT_DEV * TILE), bf16),
        in_specs=[sm, vm, vm, vm],
        out_specs=vm,
        scratch_shapes=[
            pltpu.VMEM((NT, TILE, TILE), f32),
            pltpu.VMEM((RT_DEV * TILE, TILE), f32),
            pltpu.VMEM((CT_DEV, TILE), f32),
            pltpu.SMEM((NT,), i32),
        ],
        compiler_params=pltpu.CompilerParams(vmem_limit_bytes=30 * MIB + n * MIB // 10),
        name="pmi",
    )(meta, words, row_tot, col_totals.reshape(CT_DEV, TILE))
    rows, cols = pmi.shape
    sk = sketch.shape[1]
    ch, cz, nk = rows // nc, cols // nr, nc // 2
    return pl.pallas_call(
        functools.partial(sketch_kernel, nr, nc, 1.0 / math.sqrt(rows * nr)),
        out_shape=(
            jax.ShapeDtypeStruct((rows, sk), bf16),
            jax.ShapeDtypeStruct((cols, sk), bf16),
        ),
        in_specs=[vm, vm],
        out_specs=(vm, vm),
        scratch_shapes=[pltpu.VMEM((nk, ch, sk), f32)] * 4
        + [
            pltpu.VMEM((rows, sk), bf16),
            pltpu.VMEM((sk, cols), f32),
            pltpu.VMEM((nr, sk, cz), i16),
            pltpu.VMEM((nr, sk, cz), i16),
            pltpu.VMEM((nr, 8, cz), f32),
            pltpu.VMEM((nr, 8, cz), f32),
            pltpu.VMEM((cols, sk), bf16),
        ]
        + [dma((nk,))] * 8 + [dma((nr,))] * 6,
        compiler_params=pltpu.CompilerParams(has_side_effects=True, vmem_limit_bytes=24 * MIB),
        name="sketch",
    )(pmi, sketch)


def solution(mesh):
    placed = (
        P(("row", "col"), None, None, None, None),
        P(("row", "col"), None, None),
        P(("row", "col"), None),
        P("row"),
        P("col"),
        P("col", None),
    )
    return jax.shard_map(
        functools.partial(on_device, mesh.shape["row"], mesh.shape["col"]),
        mesh=mesh,
        in_specs=placed,
        out_specs=(P("row", None), P("col", None)),
        check_vma=False,
    )
```

```python
import functools
import math

import jax
import jax.numpy as jnp
from jax import lax
from jax.experimental import pallas as pl
from jax.experimental.pallas import tpu as pltpu
from jax.sharding import PartitionSpec as P

TILE = 128
RT_DEV = 16
CT_DEV = 16
NT = RT_DEV * CT_DEV
LOW = 2
CUTS = 8 // LOW
CUT = TILE // CUTS
MASK = 2**LOW - 1
SHIFT = 0.25
CODE = (2.0 ** (16 + LOW) - 6.0) / math.sqrt(30.0)
TOP = 32766.0
MESH = pl.DeviceIdType.MESH
MIB = 1024 * 1024


def exchange_kernel(nr, nc, source, places, used, row_tot, words_out, meta_out, row_inv,
                    counts, send, meta, sem_s, sem_r, msem_s, msem_r, csem, lsem):
    n = nr * nc
    hr = nr // 2
    my_r = lax.axis_index("row")
    my_c = lax.axis_index("col")
    me = my_r * nc + my_c
    part = jnp.sum(row_tot[...])
    lane = lax.broadcasted_iota(jnp.int32, (1, TILE), 1)

    def pack(o):
        low = None
        for h in range(2):
            y = counts[o, h]
            r = lax.rsqrt(y)
            t = y * r
            t = t + 0.5 * r * (y - t * t)
            v = jnp.round(t * CODE).astype(jnp.int32)
            send[o, h * TILE : (h + 1) * TILE] = ((v >> LOW) - 32768).astype(jnp.int16)
            v = v & MASK
            for g in range(CUTS):
                bits = v[g * CUT : (g + 1) * CUT] << (LOW * g + 8 * h)
                low = bits if low is None else low + bits
        send[o, 2 * TILE :] = (low - 32768).astype(jnp.int16)
        k = jnp.where(lane == 2, used[0, o], part)
        k = jnp.where(lane == 1, places[1, o], k)
        meta[o] = jnp.where(lane == 0, places[0, o], k)

    def target(i):
        q = i // 2
        side = lax.rem(my_r // hr + 1 + lax.rem(i, 2), 2)
        row = side * hr + lax.rem(my_r + q // nc, hr)
        return row, lax.rem(my_c + lax.rem(q, nc), nc)

    def copies(i):
        row, col = target(i)
        o = row * nc + col
        return o, (
            pltpu.make_async_remote_copy(
                src_ref=send.at[o], dst_ref=words_out.at[me], send_sem=sem_s.at[i],
                recv_sem=sem_r.at[i], device_id=(row, col), device_id_type=MESH),
            pltpu.make_async_remote_copy(
                src_ref=meta.at[o], dst_ref=meta_out.at[me], send_sem=msem_s.at[i],
                recv_sem=msem_r.at[i], device_id=(row, col), device_id_type=MESH),
        )

    def load(i):
        row, col = target(i)
        o = row * nc + col
        return pltpu.make_async_copy(source.at[o], counts.at[o], csem.at[i])

    def fetch(i, _):
        load(i).start()
        return 0

    lax.fori_loop(0, n, fetch, 0)

    def issue(i, _):
        o, (a, b) = copies(i)
        load(i).wait()
        pack(o)
        a.start()
        b.start()
        return 0

    def finish(i, _):
        _, (a, b) = copies(i)
        a.wait()
        b.wait()
        return 0

    issue(0, 0)
    lax.fori_loop(2, n, issue, 0)
    load(1).wait()
    pack(me)
    own = pltpu.make_async_copy(send.at[me], words_out.at[me], lsem.at[0])
    own_meta = pltpu.make_async_copy(meta.at[me], meta_out.at[me], lsem.at[1])
    own.start()
    own_meta.start()

    def rows(i, _):
        r = 1.0 / row_tot[pl.ds(i, 1), :].astype(jnp.float32)
        row_inv[pl.ds(i * TILE, TILE), :] = jnp.broadcast_to(r, (TILE, TILE)).T
        return 0

    lax.fori_loop(0, RT_DEV, rows, 0)
    finish(0, 0)
    lax.fori_loop(2, n, finish, 0)
    own.wait()
    own_meta.wait()


def pmi_kernel(nr, nc, meta, words, row_inv, col_tot, out, acc, col_f, seen, held):
    n = nr * nc

    def clear(i, _):
        for g in range(CT_DEV):
            seen[i * CT_DEV + g] = 0
        rs = pl.ds(pl.multiple_of(i * TILE, TILE), TILE)
        out[rs, :] = jnp.zeros((TILE, CT_DEV * TILE), jnp.bfloat16)
        return 0

    lax.fori_loop(0, RT_DEV, clear, 0)
    total = lax.fori_loop(0, nr, lambda a, t: t + meta[a * nc, 0, 3], jnp.int32(0))
    scale = total.astype(jnp.float32) * (1.0 / (CODE * CODE))
    col_f[...] = scale / col_tot[...].astype(jnp.float32)

    def add(s, count):
        for h in range(2):
            p = meta[s, 0, h]
            valid = h < meta[s, 0, 2]
            fresh = seen[p] == 0

            def value(g):
                low = (words[s, 2 * TILE :].astype(jnp.int32) + 32768) >> (LOW * g + 8 * h)
                from_ = slice(h * TILE + g * CUT, h * TILE + (g + 1) * CUT)
                v = (words[s, from_].astype(jnp.int32) + 32768) * (MASK + 1)
                v = (v + (low & MASK)).astype(jnp.float32)
                return v * v

            @pl.when(jnp.logical_and(valid, fresh))
            def _():
                for g in range(CUTS):
                    acc[p, g * CUT : (g + 1) * CUT] = value(g)
                seen[p] = 1
                held[count] = p

            @pl.when(jnp.logical_and(valid, jnp.logical_not(fresh)))
            def _():
                for g in range(CUTS):
                    at = slice(g * CUT, (g + 1) * CUT)
                    acc[p, at] = acc[p, at] + value(g)

            count = count + jnp.where(jnp.logical_and(valid, fresh), 1, 0)

        return count

    count = lax.fori_loop(0, n, add, jnp.int32(0))

    def tile(i, _):
        p = held[i]
        tr = p // CT_DEV
        tc = lax.rem(p, CT_DEV)
        rs = pl.ds(pl.multiple_of(tr * TILE, TILE), TILE)
        cs = pl.ds(pl.multiple_of(tc * TILE, TILE), TILE)
        x = acc[p] * row_inv[rs, :] * col_f[pl.ds(tc, 1), :]
        out[rs, cs] = jnp.maximum(jnp.log(1.0 + x) - SHIFT, 0.0).astype(jnp.bfloat16)
        return 0

    lax.fori_loop(0, count, tile, 0)


def sketch_kernel(nr, nc, inv, pmi, sketch, rr_out, co_out, pa, ra, p1, r1, rr, rt, own_co, p2, r2,
                  f2, g2, co, sas, sar, s1s, s1r, s2s, s2r, sfs, sfr, s3s, s3r, s5s, s5r,
                  s4s, s4r):
    my_r = lax.axis_index("row")
    my_c = lax.axis_index("col")
    nk = nc // 2
    k = my_c // 2
    core = lax.rem(my_c, 2)
    other = 1 - core
    ch = pmi.shape[0] // nc
    cz = pmi.shape[1] // nr

    def rows_of(j):
        return pl.ds(pl.multiple_of(j * ch, ch), ch)

    def cols_of(j):
        return pl.ds(pl.multiple_of(j * cz, cz), cz)

    def remote(src, dst, a, b, to):
        return pltpu.make_async_remote_copy(
            src_ref=src, dst_ref=dst, send_sem=a, recv_sem=b, device_id=to,
            device_id_type=MESH)

    sibling = (my_r, k * 2 + other)

    def chip(d):
        return (my_r, lax.rem(k + d, nk) * 2 + core)

    def to_sibling(d):
        return remote(pa.at[d], ra.at[d], sas.at[d], sar.at[d], sibling)

    def rs_col(d):
        return remote(p1.at[d], r1.at[d], s1s.at[d], s1r.at[d], chip(d))

    def ag_col(d):
        mine = rr.at[rows_of(my_c)]
        return remote(mine, mine, s2s.at[d], s2r.at[d], chip(d))

    def origin(d):
        return lax.rem(k - d + nk, nk) * 2

    def forward(d):
        block = rr.at[rows_of(origin(d) + core)]
        return remote(block, block, sfs.at[d], sfr.at[d], sibling)

    def row_peer(d):
        return (lax.rem(my_r + d, nr), my_c)

    def rs_row(d):
        return (
            remote(p2.at[d], r2.at[d], s3s.at[d], s3r.at[d], row_peer(d)),
            remote(f2.at[d], g2.at[d], s5s.at[d], s5r.at[d], row_peer(d)),
        )

    def ag_row(d):
        mine = co.at[cols_of(my_r)]
        return remote(mine, mine, s4s.at[d], s4r.at[d], row_peer(d))

    def product(j):
        return jnp.dot(pmi[rows_of(j), :], sketch[...], preferred_element_type=jnp.float32)

    def zeroth(i, _):
        d = lax.rem(i + 1, nk)
        pa[d] = product(lax.rem(k + d, nk) * 2 + other)
        to_sibling(d).start()
        return 0

    lax.fori_loop(0, nk, zeroth, 0)

    def first(i, _):
        d = i + 1
        mine = product(lax.rem(k + d, nk) * 2 + core)
        to_sibling(d).wait_recv()
        p1[d] = mine + ra[d]
        rs_col(d).start()
        return 0

    lax.fori_loop(0, nk - 1, first, 0)
    own = product(my_c)
    to_sibling(0).wait_recv()
    p1[0] = own + ra[0]

    def gather(i, _):
        rs_col(i + 1).wait_recv()
        p1[0] = p1[0] + r1[i + 1]
        return 0

    lax.fori_loop(0, nk - 1, gather, 0)
    rr[rows_of(my_c), :] = p1[0].astype(jnp.bfloat16)

    def spread(i, _):
        ag_col(i + 1).start()
        return 0

    lax.fori_loop(0, nk - 1, spread, 0)
    forward(0).start()

    def turn(j):
        block = rr[rows_of(j), :].astype(jnp.float32)
        rt[:, rows_of(j)] = block.T.astype(jnp.bfloat16)

    turn(my_c)
    forward(0).wait_recv()
    turn(k * 2 + other)

    def second(i, _):
        d = i + 1
        ag_col(d).wait_recv()
        forward(d).start()
        turn(origin(d) + core)
        return 0

    lax.fori_loop(0, nk - 1, second, 0)

    def second_half(i, _):
        d = i + 1
        forward(d).wait_recv()
        turn(origin(d) + other)
        return 0

    lax.fori_loop(0, nk - 1, second_half, 0)

    def turned(j):
        return jnp.dot(rt[...], pmi[:, cols_of(j)], preferred_element_type=jnp.float32)

    def third(i, _):
        d = i + 1
        a = turned(lax.rem(my_r + d, nr))
        m = jnp.max(jnp.abs(a), axis=0, keepdims=True)
        up = jnp.where(m > 1e-30, TOP / jnp.maximum(m, 1e-30), 0.0)
        p2[d] = jnp.round(a * up).astype(jnp.int32).astype(jnp.int16)
        f2[d] = jnp.broadcast_to(m * (1.0 / TOP), (8, cz))
        a, b = rs_row(d)
        a.start()
        b.start()
        return 0

    lax.fori_loop(0, nr - 1, third, 0)
    own_co[...] = turned(my_r)

    def sent(i, _):
        d = i + 1
        rs_col(d).wait_send()
        ag_col(d).wait_send()
        to_sibling(d).wait_send()
        forward(d).wait_send()
        return 0

    lax.fori_loop(0, nk - 1, sent, 0)
    to_sibling(0).wait_send()
    forward(0).wait_send()
    rr_out[...] = rr[...]
    mine = cols_of(my_r)

    def fourth(i, _):
        d = i + 1
        a, b = rs_row(d)
        a.wait()
        b.wait()
        own_co[...] += r2[d].astype(jnp.int32).astype(jnp.float32) * g2[d, 0:1, :]
        return 0

    lax.fori_loop(0, nr - 1, fourth, 0)
    co[mine, :] = (own_co[...].T * inv).astype(jnp.bfloat16)

    def fifth(i, _):
        ag_row(i + 1).start()
        return 0

    lax.fori_loop(0, nr - 1, fifth, 0)

    def sixth(i, _):
        ag_row(i + 1).wait()
        return 0

    lax.fori_loop(0, nr - 1, sixth, 0)
    co_out[...] = co[...]


def on_device(nr, nc, pair_counts, tile_index, slot_counts, row_totals, col_totals, sketch):
    n = nr * nc
    vm = pl.BlockSpec(memory_space=pltpu.VMEM)
    sm = pl.BlockSpec(memory_space=pltpu.SMEM)
    hbm = pl.BlockSpec(memory_space=pl.ANY)
    dma = pltpu.SemaphoreType.DMA
    f32, bf16, i16, i32 = jnp.float32, jnp.bfloat16, jnp.int16, jnp.int32
    row_tot = row_totals.reshape(RT_DEV, TILE)
    words_rows = 2 * TILE + CUT
    rows, cols = RT_DEV * TILE, CT_DEV * TILE
    words, meta, row_inv = pl.pallas_call(
        functools.partial(exchange_kernel, nr, nc),
        out_shape=(
            jax.ShapeDtypeStruct((n, words_rows, TILE), i16),
            jax.ShapeDtypeStruct((n, 1, TILE), i32),
            jax.ShapeDtypeStruct((rows, TILE), f32),
        ),
        in_specs=[hbm, sm, sm, vm],
        out_specs=(hbm, hbm, vm),
        scratch_shapes=[
            pltpu.VMEM((n, 2, TILE, TILE), f32),
            pltpu.VMEM((n, words_rows, TILE), i16),
            pltpu.VMEM((n, 1, TILE), i32),
        ]
        + [dma((n,))] * 5 + [dma((2,))],
        compiler_params=pltpu.CompilerParams(has_side_effects=True, vmem_limit_bytes=56 * MIB),
        name="exchange",
    )(pair_counts[0], tile_index[0].T, slot_counts, row_tot)
    pmi = pl.pallas_call(
        functools.partial(pmi_kernel, nr, nc),
        out_shape=jax.ShapeDtypeStruct((rows, cols), bf16),
        in_specs=[sm, vm, vm, vm],
        out_specs=vm,
        scratch_shapes=[
            pltpu.VMEM((NT, TILE, TILE), f32),
            pltpu.VMEM((CT_DEV, TILE), f32),
            pltpu.SMEM((NT,), i32),
            pltpu.SMEM((NT,), i32),
        ],
        compiler_params=pltpu.CompilerParams(vmem_limit_bytes=30 * MIB + n * MIB // 10),
        name="pmi",
    )(meta, words, row_inv, col_totals.reshape(CT_DEV, TILE))
    sk = sketch.shape[1]
    ch, cz, nk = rows // nc, cols // nr, nc // 2
    return pl.pallas_call(
        functools.partial(sketch_kernel, nr, nc, 1.0 / math.sqrt(rows * nr)),
        out_shape=(
            jax.ShapeDtypeStruct((rows, sk), bf16),
            jax.ShapeDtypeStruct((cols, sk), bf16),
        ),
        in_specs=[vm, vm],
        out_specs=(vm, vm),
        scratch_shapes=[pltpu.VMEM((nk, ch, sk), f32)] * 4
        + [
            pltpu.VMEM((rows, sk), bf16),
            pltpu.VMEM((sk, rows), bf16),
            pltpu.VMEM((sk, cz), f32),
            pltpu.VMEM((nr, sk, cz), i16),
            pltpu.VMEM((nr, sk, cz), i16),
            pltpu.VMEM((nr, 8, cz), f32),
            pltpu.VMEM((nr, 8, cz), f32),
            pltpu.VMEM((cols, sk), bf16),
        ]
        + [dma((nk,))] * 8 + [dma((nr,))] * 6,
        compiler_params=pltpu.CompilerParams(has_side_effects=True, vmem_limit_bytes=24 * MIB),
        name="sketch",
    )(pmi, sketch)


def solution(mesh):
    placed = (
        P(("row", "col"), None, None, None, None),
        P(("row", "col"), None, None),
        P(("row", "col"), None),
        P("row"),
        P("col"),
        P("col", None),
    )
    return jax.shard_map(
        functools.partial(on_device, mesh.shape["row"], mesh.shape["col"]),
        mesh=mesh,
        in_specs=placed,
        out_specs=(P("row", None), P("col", None)),
        check_vma=False,
    )
```

```python
import functools
import math

import jax
import jax.numpy as jnp
from jax import lax
from jax.experimental import pallas as pl
from jax.experimental.pallas import tpu as pltpu
from jax.sharding import PartitionSpec as P

TILE = 128
RT_DEV = 16
CT_DEV = 16
NT = RT_DEV * CT_DEV
LOW = 2
CUTS = 8 // LOW
CUT = TILE // CUTS
MASK = 2**LOW - 1
SHIFT = 0.25
CODE = (2.0 ** (16 + LOW) - 10.0) / (30.0**0.25 - 0.01**0.25)
BASE = math.floor(0.01**0.25 * CODE) - 4
TOP = 32766.0
MESH = pl.DeviceIdType.MESH
MIB = 1024 * 1024


def exchange_kernel(nr, nc, source, places, used, row_tot, words_out, meta_out, row_inv,
                    counts, send, meta, sem_s, sem_r, msem_s, msem_r, csem, lsem):
    n = nr * nc
    hr = nr // 2
    my_r = lax.axis_index("row")
    my_c = lax.axis_index("col")
    me = my_r * nc + my_c
    part = jnp.sum(row_tot[...])
    lane = lax.broadcasted_iota(jnp.int32, (1, TILE), 1)

    def root(y):
        r = lax.rsqrt(y)
        t = y * r
        return t + 0.5 * r * (y - t * t)

    def pack(o):
        low = None
        for h in range(2):
            t = root(root(counts[o, h]))
            v = jnp.round(t * CODE - BASE).astype(jnp.int32)
            send[o, h * TILE : (h + 1) * TILE] = ((v >> LOW) - 32768).astype(jnp.int16)
            v = v & MASK
            for g in range(CUTS):
                bits = v[g * CUT : (g + 1) * CUT] << (LOW * g + 8 * h)
                low = bits if low is None else low + bits
        send[o, 2 * TILE :] = (low - 32768).astype(jnp.int16)
        k = jnp.where(lane == 2, used[0, o], part)
        k = jnp.where(lane == 1, places[1, o], k)
        meta[o] = jnp.where(lane == 0, places[0, o], k)

    def target(i):
        q = i // 2
        side = lax.rem(my_r // hr + 1 + lax.rem(i, 2), 2)
        row = side * hr + lax.rem(my_r + q // nc, hr)
        return row, lax.rem(my_c + lax.rem(q, nc), nc)

    def copies(i):
        row, col = target(i)
        o = row * nc + col
        return o, (
            pltpu.make_async_remote_copy(
                src_ref=send.at[o], dst_ref=words_out.at[me], send_sem=sem_s.at[i],
                recv_sem=sem_r.at[i], device_id=(row, col), device_id_type=MESH),
            pltpu.make_async_remote_copy(
                src_ref=meta.at[o], dst_ref=meta_out.at[me], send_sem=msem_s.at[i],
                recv_sem=msem_r.at[i], device_id=(row, col), device_id_type=MESH),
        )

    def load(i):
        row, col = target(i)
        o = row * nc + col
        return pltpu.make_async_copy(source.at[o], counts.at[o], csem.at[i])

    def fetch(i, _):
        load(i).start()
        return 0

    lax.fori_loop(0, n, fetch, 0)

    def issue(i, _):
        o, (a, b) = copies(i)
        load(i).wait()
        pack(o)
        a.start()
        b.start()
        return 0

    def finish(i, _):
        _, (a, b) = copies(i)
        a.wait()
        b.wait()
        return 0

    issue(0, 0)
    lax.fori_loop(2, n, issue, 0)
    load(1).wait()
    pack(me)
    own = pltpu.make_async_copy(send.at[me], words_out.at[me], lsem.at[0])
    own_meta = pltpu.make_async_copy(meta.at[me], meta_out.at[me], lsem.at[1])
    own.start()
    own_meta.start()

    def rows(i, _):
        r = 1.0 / row_tot[pl.ds(i, 1), :].astype(jnp.float32)
        row_inv[pl.ds(i * TILE, TILE), :] = jnp.broadcast_to(r, (TILE, TILE)).T
        return 0

    lax.fori_loop(0, RT_DEV, rows, 0)
    finish(0, 0)
    lax.fori_loop(2, n, finish, 0)
    own.wait()
    own_meta.wait()


def pmi_kernel(nr, nc, meta, words, row_inv, col_tot, out, acc, col_f, seen, held):
    n = nr * nc

    def clear(i, _):
        for g in range(CT_DEV):
            seen[i * CT_DEV + g] = 0
        rs = pl.ds(pl.multiple_of(i * TILE, TILE), TILE)
        out[rs, :] = jnp.zeros((TILE, CT_DEV * TILE), jnp.bfloat16)
        return 0

    lax.fori_loop(0, RT_DEV, clear, 0)
    total = lax.fori_loop(0, nr, lambda a, t: t + meta[a * nc, 0, 3], jnp.int32(0))
    col_f[...] = total.astype(jnp.float32) / col_tot[...].astype(jnp.float32)

    def add(s, count):
        for h in range(2):
            p = meta[s, 0, h]
            valid = h < meta[s, 0, 2]
            fresh = seen[p] == 0

            def value(g):
                low = (words[s, 2 * TILE :].astype(jnp.int32) + 32768) >> (LOW * g + 8 * h)
                from_ = slice(h * TILE + g * CUT, h * TILE + (g + 1) * CUT)
                v = (words[s, from_].astype(jnp.int32) + 32768) * (MASK + 1)
                v = (v + (low & MASK) + BASE).astype(jnp.float32) * (1.0 / CODE)
                v = v * v
                return v * v

            @pl.when(jnp.logical_and(valid, fresh))
            def _():
                for g in range(CUTS):
                    acc[p, g * CUT : (g + 1) * CUT] = value(g)
                seen[p] = 1
                held[count] = p

            @pl.when(jnp.logical_and(valid, jnp.logical_not(fresh)))
            def _():
                for g in range(CUTS):
                    at = slice(g * CUT, (g + 1) * CUT)
                    acc[p, at] = acc[p, at] + value(g)

            count = count + jnp.where(jnp.logical_and(valid, fresh), 1, 0)

        return count

    count = lax.fori_loop(0, n, add, jnp.int32(0))

    def tile(i, _):
        p = held[i]
        tr = p // CT_DEV
        tc = lax.rem(p, CT_DEV)
        rs = pl.ds(pl.multiple_of(tr * TILE, TILE), TILE)
        cs = pl.ds(pl.multiple_of(tc * TILE, TILE), TILE)
        x = acc[p] * row_inv[rs, :] * col_f[pl.ds(tc, 1), :]
        out[rs, cs] = jnp.maximum(jnp.log(1.0 + x) - SHIFT, 0.0).astype(jnp.bfloat16)
        return 0

    lax.fori_loop(0, count, tile, 0)


def sketch_kernel(nr, nc, inv, pmi, sketch, rr_out, co_out, pa, ra, p1, r1, rr, rt, own_co, p2, r2,
                  f2, g2, co, sas, sar, s1s, s1r, s2s, s2r, sfs, sfr, s3s, s3r, s5s, s5r,
                  s4s, s4r):
    my_r = lax.axis_index("row")
    my_c = lax.axis_index("col")
    nk = nc // 2
    k = my_c // 2
    core = lax.rem(my_c, 2)
    other = 1 - core
    ch = pmi.shape[0] // nc
    cz = pmi.shape[1] // nr

    def rows_of(j):
        return pl.ds(pl.multiple_of(j * ch, ch), ch)

    def cols_of(j):
        return pl.ds(pl.multiple_of(j * cz, cz), cz)

    def remote(src, dst, a, b, to):
        return pltpu.make_async_remote_copy(
            src_ref=src, dst_ref=dst, send_sem=a, recv_sem=b, device_id=to,
            device_id_type=MESH)

    sibling = (my_r, k * 2 + other)

    def chip(d):
        return (my_r, lax.rem(k + d, nk) * 2 + core)

    def to_sibling(d):
        return remote(pa.at[d], ra.at[d], sas.at[d], sar.at[d], sibling)

    def rs_col(d):
        return remote(p1.at[d], r1.at[d], s1s.at[d], s1r.at[d], chip(d))

    def ag_col(d):
        mine = rr.at[rows_of(my_c)]
        return remote(mine, mine, s2s.at[d], s2r.at[d], chip(d))

    def origin(d):
        return lax.rem(k - d + nk, nk) * 2

    def forward(d):
        block = rr.at[rows_of(origin(d) + core)]
        return remote(block, block, sfs.at[d], sfr.at[d], sibling)

    def row_peer(d):
        return (lax.rem(my_r + d, nr), my_c)

    def rs_row(d):
        return (
            remote(p2.at[d], r2.at[d], s3s.at[d], s3r.at[d], row_peer(d)),
            remote(f2.at[d], g2.at[d], s5s.at[d], s5r.at[d], row_peer(d)),
        )

    def ag_row(d):
        mine = co.at[cols_of(my_r)]
        return remote(mine, mine, s4s.at[d], s4r.at[d], row_peer(d))

    def product(j):
        return jnp.dot(pmi[rows_of(j), :], sketch[...], preferred_element_type=jnp.float32)

    barrier = pltpu.get_barrier_semaphore()

    def greet(to):
        pl.semaphore_signal(barrier, inc=1, device_id=to, device_id_type=MESH)

    greet(sibling)
    for d in range(1, nk):
        greet(chip(d))
    for d in range(1, nr):
        greet(row_peer(d))
    pl.semaphore_wait(barrier, nk + nr - 1)

    def zeroth(i, _):
        d = lax.rem(i + 1, nk)
        pa[d] = product(lax.rem(k + d, nk) * 2 + other)
        to_sibling(d).start()
        return 0

    lax.fori_loop(0, nk, zeroth, 0)

    def first(i, _):
        d = i + 1
        mine = product(lax.rem(k + d, nk) * 2 + core)
        to_sibling(d).wait_recv()
        p1[d] = mine + ra[d]
        rs_col(d).start()
        return 0

    lax.fori_loop(0, nk - 1, first, 0)
    own = product(my_c)
    to_sibling(0).wait_recv()
    p1[0] = own + ra[0]

    def gather(i, _):
        rs_col(i + 1).wait_recv()
        p1[0] = p1[0] + r1[i + 1]
        return 0

    lax.fori_loop(0, nk - 1, gather, 0)
    rr[rows_of(my_c), :] = p1[0].astype(jnp.bfloat16)

    def spread(i, _):
        ag_col(i + 1).start()
        return 0

    lax.fori_loop(0, nk - 1, spread, 0)
    forward(0).start()

    def turn(j):
        block = rr[rows_of(j), :].astype(jnp.float32)
        rt[:, rows_of(j)] = block.T.astype(jnp.bfloat16)

    turn(my_c)
    forward(0).wait_recv()
    turn(k * 2 + other)

    def second(i, _):
        d = i + 1
        ag_col(d).wait_recv()
        forward(d).start()
        turn(origin(d) + core)
        return 0

    lax.fori_loop(0, nk - 1, second, 0)

    def second_half(i, _):
        d = i + 1
        forward(d).wait_recv()
        turn(origin(d) + other)
        return 0

    lax.fori_loop(0, nk - 1, second_half, 0)

    def turned(j):
        return jnp.dot(rt[...], pmi[:, cols_of(j)], preferred_element_type=jnp.float32)

    def third(i, _):
        d = i + 1
        a = turned(lax.rem(my_r + d, nr))
        m = jnp.max(jnp.abs(a), axis=0, keepdims=True)
        up = jnp.where(m > 1e-30, TOP / jnp.maximum(m, 1e-30), 0.0)
        p2[d] = jnp.round(a * up).astype(jnp.int32).astype(jnp.int16)
        f2[d] = jnp.broadcast_to(m * (1.0 / TOP), (8, cz))
        a, b = rs_row(d)
        a.start()
        b.start()
        return 0

    lax.fori_loop(0, nr - 1, third, 0)
    own_co[...] = turned(my_r)

    def sent(i, _):
        d = i + 1
        rs_col(d).wait_send()
        ag_col(d).wait_send()
        to_sibling(d).wait_send()
        forward(d).wait_send()
        return 0

    lax.fori_loop(0, nk - 1, sent, 0)
    to_sibling(0).wait_send()
    forward(0).wait_send()
    rr_out[...] = rr[...]
    mine = cols_of(my_r)

    def fourth(i, _):
        d = i + 1
        a, b = rs_row(d)
        a.wait()
        b.wait()
        own_co[...] += r2[d].astype(jnp.int32).astype(jnp.float32) * g2[d, 0:1, :]
        return 0

    lax.fori_loop(0, nr - 1, fourth, 0)
    co[mine, :] = (own_co[...].T * inv).astype(jnp.bfloat16)

    def fifth(i, _):
        ag_row(i + 1).start()
        return 0

    lax.fori_loop(0, nr - 1, fifth, 0)

    def sixth(i, _):
        ag_row(i + 1).wait()
        return 0

    lax.fori_loop(0, nr - 1, sixth, 0)
    co_out[...] = co[...]


def on_device(nr, nc, pair_counts, tile_index, slot_counts, row_totals, col_totals, sketch):
    n = nr * nc
    vm = pl.BlockSpec(memory_space=pltpu.VMEM)
    sm = pl.BlockSpec(memory_space=pltpu.SMEM)
    hbm = pl.BlockSpec(memory_space=pl.ANY)
    dma = pltpu.SemaphoreType.DMA
    f32, bf16, i16, i32 = jnp.float32, jnp.bfloat16, jnp.int16, jnp.int32
    row_tot = row_totals.reshape(RT_DEV, TILE)
    words_rows = 2 * TILE + CUT
    rows, cols = RT_DEV * TILE, CT_DEV * TILE
    words, meta, row_inv = pl.pallas_call(
        functools.partial(exchange_kernel, nr, nc),
        out_shape=(
            jax.ShapeDtypeStruct((n, words_rows, TILE), i16),
            jax.ShapeDtypeStruct((n, 1, TILE), i32),
            jax.ShapeDtypeStruct((rows, TILE), f32),
        ),
        in_specs=[hbm, sm, sm, vm],
        out_specs=(hbm, hbm, vm),
        scratch_shapes=[
            pltpu.VMEM((n, 2, TILE, TILE), f32),
            pltpu.VMEM((n, words_rows, TILE), i16),
            pltpu.VMEM((n, 1, TILE), i32),
        ]
        + [dma((n,))] * 5 + [dma((2,))],
        compiler_params=pltpu.CompilerParams(has_side_effects=True, vmem_limit_bytes=48 * MIB),
        name="exchange",
    )(pair_counts[0], tile_index[0].T, slot_counts, row_tot)
    pmi = pl.pallas_call(
        functools.partial(pmi_kernel, nr, nc),
        out_shape=jax.ShapeDtypeStruct((rows, cols), bf16),
        in_specs=[sm, vm, vm, vm],
        out_specs=vm,
        scratch_shapes=[
            pltpu.VMEM((NT, TILE, TILE), f32),
            pltpu.VMEM((CT_DEV, TILE), f32),
            pltpu.SMEM((NT,), i32),
            pltpu.SMEM((NT,), i32),
        ],
        compiler_params=pltpu.CompilerParams(vmem_limit_bytes=30 * MIB + n * MIB // 10),
        name="pmi",
    )(meta, words, row_inv, col_totals.reshape(CT_DEV, TILE))
    sk = sketch.shape[1]
    ch, cz, nk = rows // nc, cols // nr, nc // 2
    return pl.pallas_call(
        functools.partial(sketch_kernel, nr, nc, 1.0 / math.sqrt(rows * nr)),
        out_shape=(
            jax.ShapeDtypeStruct((rows, sk), bf16),
            jax.ShapeDtypeStruct((cols, sk), bf16),
        ),
        in_specs=[vm, vm],
        out_specs=(vm, vm),
        scratch_shapes=[pltpu.VMEM((nk, ch, sk), f32)] * 4
        + [
            pltpu.VMEM((rows, sk), bf16),
            pltpu.VMEM((sk, rows), bf16),
            pltpu.VMEM((sk, cz), f32),
            pltpu.VMEM((nr, sk, cz), i16),
            pltpu.VMEM((nr, sk, cz), i16),
            pltpu.VMEM((nr, 8, cz), f32),
            pltpu.VMEM((nr, 8, cz), f32),
            pltpu.VMEM((cols, sk), bf16),
        ]
        + [dma((nk,))] * 8 + [dma((nr,))] * 6,
        compiler_params=pltpu.CompilerParams(
            has_side_effects=True, vmem_limit_bytes=24 * MIB, collective_id=1),
        name="sketch",
    )(pmi, sketch)


def solution(mesh):
    placed = (
        P(("row", "col"), None, None, None, None),
        P(("row", "col"), None, None),
        P(("row", "col"), None),
        P("row"),
        P("col"),
        P("col", None),
    )
    return jax.shard_map(
        functools.partial(on_device, mesh.shape["row"], mesh.shape["col"]),
        mesh=mesh,
        in_specs=placed,
        out_specs=(P("row", None), P("col", None)),
        check_vma=False,
    )
```

```python
import functools
import math

import jax
import jax.numpy as jnp
from jax import lax
from jax.experimental import pallas as pl
from jax.experimental.pallas import tpu as pltpu
from jax.sharding import PartitionSpec as P

TILE = 128
RT_DEV = 16
CT_DEV = 16
NT = RT_DEV * CT_DEV
LOW = 2
CUTS = 8 // LOW
CUT = TILE // CUTS
MASK = 2**LOW - 1
SHIFT = 0.25
CODE = (2.0 ** (16 + LOW) - 10.0) / (30.0**0.25 - 0.01**0.25)
BASE = math.floor(0.01**0.25 * CODE) - 4
TOP = 32766.0
MESH = pl.DeviceIdType.MESH
MIB = 1024 * 1024


def exchange_kernel(nr, nc, source, places, used, row_tot, words_out, meta_out, row_inv,
                    counts, send, meta, sem_s, sem_r, msem_s, msem_r, csem, lsem):
    n = nr * nc
    hr = nr // 2
    my_r = lax.axis_index("row")
    my_c = lax.axis_index("col")
    me = my_r * nc + my_c
    part = jnp.sum(row_tot[...])
    lane = lax.broadcasted_iota(jnp.int32, (1, TILE), 1)

    def root(y):
        r = lax.rsqrt(y)
        t = y * r
        return t + 0.5 * r * (y - t * t)

    def pack(o):
        low = None
        for h in range(2):
            t = root(root(counts[o, h]))
            v = jnp.round(t * CODE - BASE).astype(jnp.int32)
            send[o, h * TILE : (h + 1) * TILE] = ((v >> LOW) - 32768).astype(jnp.int16)
            v = v & MASK
            for g in range(CUTS):
                bits = v[g * CUT : (g + 1) * CUT] << (LOW * g + 8 * h)
                low = bits if low is None else low + bits
        send[o, 2 * TILE :] = (low - 32768).astype(jnp.int16)
        k = jnp.where(lane == 2, used[0, o], part)
        k = jnp.where(lane == 1, places[1, o], k)
        meta[o] = jnp.where(lane == 0, places[0, o], k)

    def target(i):
        q = i // 2
        side = lax.rem(my_r // hr + 1 + lax.rem(i, 2), 2)
        row = side * hr + lax.rem(my_r + q // nc, hr)
        return row, lax.rem(my_c + lax.rem(q, nc), nc)

    def copies(i):
        row, col = target(i)
        o = row * nc + col
        return o, (
            pltpu.make_async_remote_copy(
                src_ref=send.at[o], dst_ref=words_out.at[me], send_sem=sem_s.at[i],
                recv_sem=sem_r.at[i], device_id=(row, col), device_id_type=MESH),
            pltpu.make_async_remote_copy(
                src_ref=meta.at[o], dst_ref=meta_out.at[me], send_sem=msem_s.at[i],
                recv_sem=msem_r.at[i], device_id=(row, col), device_id_type=MESH),
        )

    def load(i):
        row, col = target(i)
        o = row * nc + col
        return pltpu.make_async_copy(source.at[o], counts.at[o], csem.at[i])

    def fetch(i, _):
        load(i).start()
        return 0

    lax.fori_loop(0, n, fetch, 0)

    def issue(i, _):
        o, (a, b) = copies(i)
        load(i).wait()
        pack(o)
        a.start()
        b.start()
        return 0

    def finish(i, _):
        _, (a, b) = copies(i)
        a.wait()
        b.wait()
        return 0

    issue(0, 0)
    lax.fori_loop(2, n, issue, 0)
    load(1).wait()
    pack(me)
    own = pltpu.make_async_copy(send.at[me], words_out.at[me], lsem.at[0])
    own_meta = pltpu.make_async_copy(meta.at[me], meta_out.at[me], lsem.at[1])
    own.start()
    own_meta.start()

    def rows(i, _):
        r = 1.0 / row_tot[pl.ds(i, 1), :].astype(jnp.float32)
        row_inv[pl.ds(i * TILE, TILE), :] = jnp.broadcast_to(r, (TILE, TILE)).T
        return 0

    lax.fori_loop(0, RT_DEV, rows, 0)
    finish(0, 0)
    lax.fori_loop(2, n, finish, 0)
    own.wait()
    own_meta.wait()


def pmi_kernel(nr, nc, meta, words, row_inv, col_tot, out, acc, col_f, seen, held):
    n = nr * nc

    def clear(i, _):
        for g in range(CT_DEV):
            seen[i * CT_DEV + g] = 0
        rs = pl.ds(pl.multiple_of(i * TILE, TILE), TILE)
        out[rs, :] = jnp.zeros((TILE, CT_DEV * TILE), jnp.bfloat16)
        return 0

    lax.fori_loop(0, RT_DEV, clear, 0)
    total = lax.fori_loop(0, nr, lambda a, t: t + meta[a * nc, 0, 3], jnp.int32(0))
    col_f[...] = total.astype(jnp.float32) / col_tot[...].astype(jnp.float32)

    def add(s, count):
        for h in range(2):
            p = meta[s, 0, h]
            valid = h < meta[s, 0, 2]
            fresh = seen[p] == 0

            def value(g):
                low = (words[s, 2 * TILE :].astype(jnp.int32) + 32768) >> (LOW * g + 8 * h)
                from_ = slice(h * TILE + g * CUT, h * TILE + (g + 1) * CUT)
                v = (words[s, from_].astype(jnp.int32) + 32768) * (MASK + 1)
                v = (v + (low & MASK) + BASE).astype(jnp.float32) * (1.0 / CODE)
                v = v * v
                return v * v

            @pl.when(jnp.logical_and(valid, fresh))
            def _():
                for g in range(CUTS):
                    acc[p, g * CUT : (g + 1) * CUT] = value(g)
                seen[p] = 1
                held[count] = p

            @pl.when(jnp.logical_and(valid, jnp.logical_not(fresh)))
            def _():
                for g in range(CUTS):
                    at = slice(g * CUT, (g + 1) * CUT)
                    acc[p, at] = acc[p, at] + value(g)

            count = count + jnp.where(jnp.logical_and(valid, fresh), 1, 0)

        return count

    count = lax.fori_loop(0, n, add, jnp.int32(0))

    def tile(i, _):
        p = held[i]
        tr = p // CT_DEV
        tc = lax.rem(p, CT_DEV)
        rs = pl.ds(pl.multiple_of(tr * TILE, TILE), TILE)
        cs = pl.ds(pl.multiple_of(tc * TILE, TILE), TILE)
        x = acc[p] * row_inv[rs, :] * col_f[pl.ds(tc, 1), :]
        out[rs, cs] = jnp.maximum(jnp.log(1.0 + x) - SHIFT, 0.0).astype(jnp.bfloat16)
        return 0

    lax.fori_loop(0, count, tile, 0)


def sketch_kernel(nr, nc, inv, pmi, sketch, rr_out, co_out, pa, ra, p1, r1, rr, rt, own_co, p2, r2,
                  f2, g2, co, sas, sar, s1s, s1r, s2s, s2r, sfs, sfr, s3s, s3r, s5s, s5r,
                  s4s, s4r, s6s, s6r):
    my_r = lax.axis_index("row")
    my_c = lax.axis_index("col")
    nk = nc // 2
    k = my_c // 2
    core = lax.rem(my_c, 2)
    other = 1 - core
    ch = pmi.shape[0] // nc
    cz = pmi.shape[1] // nr

    def rows_of(j):
        return pl.ds(pl.multiple_of(j * ch, ch), ch)

    def cols_of(j):
        return pl.ds(pl.multiple_of(j * cz, cz), cz)

    def remote(src, dst, a, b, to):
        return pltpu.make_async_remote_copy(
            src_ref=src, dst_ref=dst, send_sem=a, recv_sem=b, device_id=to,
            device_id_type=MESH)

    sibling = (my_r, k * 2 + other)

    def chip(d):
        return (my_r, lax.rem(k + d, nk) * 2 + core)

    def to_sibling(d):
        return remote(pa.at[d], ra.at[d], sas.at[d], sar.at[d], sibling)

    def rs_col(d):
        return remote(p1.at[d], r1.at[d], s1s.at[d], s1r.at[d], chip(d))

    def ag_col(d):
        mine = rr.at[rows_of(my_c)]
        return remote(mine, mine, s2s.at[d], s2r.at[d], chip(d))

    def origin(d):
        return lax.rem(k - d + nk, nk) * 2

    def forward(d):
        block = rr.at[rows_of(origin(d) + core)]
        return remote(block, block, sfs.at[d], sfr.at[d], sibling)

    def row_peer(d):
        return (lax.rem(my_r + d, nr), my_c)

    def rs_row(d):
        return (
            remote(p2.at[d], r2.at[d], s3s.at[d], s3r.at[d], row_peer(d)),
            remote(f2.at[d], g2.at[d], s5s.at[d], s5r.at[d], row_peer(d)),
        )

    def product(j):
        return jnp.dot(pmi[rows_of(j), :], sketch[...], preferred_element_type=jnp.float32)

    barrier = pltpu.get_barrier_semaphore()

    def greet(to):
        pl.semaphore_signal(barrier, inc=1, device_id=to, device_id_type=MESH)

    greet(sibling)
    for d in range(1, nk):
        greet(chip(d))
    for d in range(1, nr):
        greet(row_peer(d))
    pl.semaphore_wait(barrier, nk + nr - 1)

    def zeroth(i, _):
        d = lax.rem(i + 1, nk)
        pa[d] = product(lax.rem(k + d, nk) * 2 + other)
        to_sibling(d).start()
        return 0

    lax.fori_loop(0, nk, zeroth, 0)

    def first(i, _):
        d = i + 1
        mine = product(lax.rem(k + d, nk) * 2 + core)
        to_sibling(d).wait_recv()
        p1[d] = mine + ra[d]
        rs_col(d).start()
        return 0

    lax.fori_loop(0, nk - 1, first, 0)
    own = product(my_c)
    to_sibling(0).wait_recv()
    p1[0] = own + ra[0]

    def gather(i, _):
        rs_col(i + 1).wait_recv()
        p1[0] = p1[0] + r1[i + 1]
        return 0

    lax.fori_loop(0, nk - 1, gather, 0)
    rr[rows_of(my_c), :] = p1[0].astype(jnp.bfloat16)

    def spread(i, _):
        ag_col(i + 1).start()
        return 0

    lax.fori_loop(0, nk - 1, spread, 0)
    forward(0).start()

    def turn(j):
        block = rr[rows_of(j), :].astype(jnp.float32)
        rt[:, rows_of(j)] = block.T.astype(jnp.bfloat16)

    turn(my_c)
    forward(0).wait_recv()
    turn(k * 2 + other)

    def second(i, _):
        d = i + 1
        ag_col(d).wait_recv()
        forward(d).start()
        turn(origin(d) + core)
        return 0

    lax.fori_loop(0, nk - 1, second, 0)

    def second_half(i, _):
        d = i + 1
        forward(d).wait_recv()
        turn(origin(d) + other)
        return 0

    lax.fori_loop(0, nk - 1, second_half, 0)

    def turned(j):
        return jnp.dot(rt[...], pmi[:, cols_of(j)], preferred_element_type=jnp.float32)

    def third(i, _):
        d = i + 1
        a = turned(lax.rem(my_r + d, nr))
        m = jnp.max(jnp.abs(a), axis=0, keepdims=True)
        up = jnp.where(m > 1e-30, TOP / jnp.maximum(m, 1e-30), 0.0)
        p2[d] = jnp.round(a * up).astype(jnp.int32).astype(jnp.int16)
        f2[d] = jnp.broadcast_to(m * (1.0 / TOP), (8, cz))
        a, b = rs_row(d)
        a.start()
        b.start()
        return 0

    lax.fori_loop(0, nr - 1, third, 0)
    own_co[...] = turned(my_r)

    def sent(i, _):
        d = i + 1
        rs_col(d).wait_send()
        ag_col(d).wait_send()
        to_sibling(d).wait_send()
        forward(d).wait_send()
        return 0

    lax.fori_loop(0, nk - 1, sent, 0)
    to_sibling(0).wait_send()
    forward(0).wait_send()
    rr_out[...] = rr[...]
    mine = cols_of(my_r)

    def fourth(i, _):
        d = i + 1
        a, b = rs_row(d)
        a.wait()
        b.wait()
        own_co[...] += r2[d].astype(jnp.int32).astype(jnp.float32) * g2[d, 0:1, :]
        return 0

    lax.fori_loop(0, nr - 1, fourth, 0)
    co[mine, :] = (own_co[...].T * inv).astype(jnp.bfloat16)

    up_ok = my_r < nr - 1
    down_ok = my_r > 0

    def ag_up(j):
        block = co.at[cols_of(j)]
        return remote(block, block, s4s.at[j], s4r.at[j], row_peer(1))

    def ag_down(j):
        block = co.at[cols_of(j)]
        return remote(block, block, s6s.at[j], s6r.at[j], row_peer(nr - 1))

    @pl.when(up_ok)
    def _():
        ag_up(my_r).start()

    @pl.when(down_ok)
    def _():
        ag_down(my_r).start()

    def fifth(i, _):
        low = my_r - 1 - i
        high = my_r + 1 + i

        @pl.when(low >= 0)
        def _():
            ag_up(low).wait_recv()

            @pl.when(up_ok)
            def _():
                ag_up(low).start()

        @pl.when(high < nr)
        def _():
            ag_down(high).wait_recv()

            @pl.when(down_ok)
            def _():
                ag_down(high).start()

        return 0

    lax.fori_loop(0, nr - 1, fifth, 0)

    def sixth(j, _):
        @pl.when(jnp.logical_and(up_ok, j <= my_r))
        def _():
            ag_up(j).wait_send()

        @pl.when(jnp.logical_and(down_ok, j >= my_r))
        def _():
            ag_down(j).wait_send()

        return 0

    lax.fori_loop(0, nr, sixth, 0)
    co_out[...] = co[...]


def on_device(nr, nc, pair_counts, tile_index, slot_counts, row_totals, col_totals, sketch):
    n = nr * nc
    vm = pl.BlockSpec(memory_space=pltpu.VMEM)
    sm = pl.BlockSpec(memory_space=pltpu.SMEM)
    hbm = pl.BlockSpec(memory_space=pl.ANY)
    dma = pltpu.SemaphoreType.DMA
    f32, bf16, i16, i32 = jnp.float32, jnp.bfloat16, jnp.int16, jnp.int32
    row_tot = row_totals.reshape(RT_DEV, TILE)
    words_rows = 2 * TILE + CUT
    rows, cols = RT_DEV * TILE, CT_DEV * TILE
    words, meta, row_inv = pl.pallas_call(
        functools.partial(exchange_kernel, nr, nc),
        out_shape=(
            jax.ShapeDtypeStruct((n, words_rows, TILE), i16),
            jax.ShapeDtypeStruct((n, 1, TILE), i32),
            jax.ShapeDtypeStruct((rows, TILE), f32),
        ),
        in_specs=[hbm, sm, sm, vm],
        out_specs=(hbm, hbm, vm),
        scratch_shapes=[
            pltpu.VMEM((n, 2, TILE, TILE), f32),
            pltpu.VMEM((n, words_rows, TILE), i16),
            pltpu.VMEM((n, 1, TILE), i32),
        ]
        + [dma((n,))] * 5 + [dma((2,))],
        compiler_params=pltpu.CompilerParams(has_side_effects=True, vmem_limit_bytes=48 * MIB),
        name="exchange",
    )(pair_counts[0], tile_index[0].T, slot_counts, row_tot)
    pmi = pl.pallas_call(
        functools.partial(pmi_kernel, nr, nc),
        out_shape=jax.ShapeDtypeStruct((rows, cols), bf16),
        in_specs=[sm, vm, vm, vm],
        out_specs=vm,
        scratch_shapes=[
            pltpu.VMEM((NT, TILE, TILE), f32),
            pltpu.VMEM((CT_DEV, TILE), f32),
            pltpu.SMEM((NT,), i32),
            pltpu.SMEM((NT,), i32),
        ],
        compiler_params=pltpu.CompilerParams(vmem_limit_bytes=30 * MIB + n * MIB // 10),
        name="pmi",
    )(meta, words, row_inv, col_totals.reshape(CT_DEV, TILE))
    sk = sketch.shape[1]
    ch, cz, nk = rows // nc, cols // nr, nc // 2
    return pl.pallas_call(
        functools.partial(sketch_kernel, nr, nc, 1.0 / math.sqrt(rows * nr)),
        out_shape=(
            jax.ShapeDtypeStruct((rows, sk), bf16),
            jax.ShapeDtypeStruct((cols, sk), bf16),
        ),
        in_specs=[vm, vm],
        out_specs=(vm, vm),
        scratch_shapes=[pltpu.VMEM((nk, ch, sk), f32)] * 4
        + [
            pltpu.VMEM((rows, sk), bf16),
            pltpu.VMEM((sk, rows), bf16),
            pltpu.VMEM((sk, cz), f32),
            pltpu.VMEM((nr, sk, cz), i16),
            pltpu.VMEM((nr, sk, cz), i16),
            pltpu.VMEM((nr, 8, cz), f32),
            pltpu.VMEM((nr, 8, cz), f32),
            pltpu.VMEM((cols, sk), bf16),
        ]
        + [dma((nk,))] * 8 + [dma((nr,))] * 8,
        compiler_params=pltpu.CompilerParams(
            has_side_effects=True, vmem_limit_bytes=24 * MIB, collective_id=1),
        name="sketch",
    )(pmi, sketch)


def solution(mesh):
    placed = (
        P(("row", "col"), None, None, None, None),
        P(("row", "col"), None, None),
        P(("row", "col"), None),
        P("row"),
        P("col"),
        P("col", None),
    )
    return jax.shard_map(
        functools.partial(on_device, mesh.shape["row"], mesh.shape["col"]),
        mesh=mesh,
        in_specs=placed,
        out_specs=(P("row", None), P("col", None)),
        check_vma=False,
    )
```
